512 devices in a mesh: aux: 32 (over z_lo, y), basis: 16 (over z_hi, x, core).
Axes of the slice: x: 4, y: 8, z: 8 (z_hi: 2, z_lo: 4; z = z_hi * 4 + z_lo), core: 2. Of those that a mesh axis runs over, the one named last changes fastest.
Arguments:
- factors: bfloat16 [128, 500, 8192], P('aux', None, 'basis'), may hold values from -0.1875 to 0.1875
Outputs:
- exchange_band: float32 [3, 8192, 512], P(None, ('basis', 'aux'))
The draws below stay inside these ranges and needn't reach their ends.
All inputs are finite; a program needn't handle non-finite values.
Results may differ from the reference program's by a relative error of at most 0.0003.
Values may be sent and summed in bfloat16 or wider, within the bound.
No kernel may reach another device: no remote copies, remote signals or barrier semaphores. Data moves between devices by JAX's collectives and lax.ppermute only.
A program may use at most 64 MiB of HBM per device.

```python
import jax
import jax.numpy as jnp
from jax import lax

NBF = 8192
NOCC = 500
P_DEV = 4
SHIFTS = 3
NAUX = 128
N_AUX = 32
N_BASIS = 16


def with_spikes(array, key, source, target, blocks, factor):
    def block_of(dim):
        return (jnp.arange(array.shape[dim]) // (array.shape[dim] // blocks)).reshape((-1,) + (1,) * (array.ndim - 1 - dim))

    near = jax.random.permutation(key, blocks)[block_of(target)]
    far = (block_of(target) + blocks // 2) % blocks
    return jnp.where((block_of(source) == near) | (block_of(source) == far), factor * array, array)


def block_levels(own_key, shape, cuts, smallest, top_value):
    gain, own = 1.0, jax.random.fold_in(own_key, 6)
    for dim, blocks in cuts:
        draws = jnp.exp(jax.random.uniform(jax.random.fold_in(own, dim), (blocks,), jnp.float32, smallest / len(cuts), top_value / len(cuts)))
        gain = gain * jnp.repeat(draws, shape[dim] // blocks).reshape([-1 if axis == dim else 1 for axis in range(len(shape))])
    return gain


def noise_with(own_key, shape, spread, most, cuts, heavy, held_as=jnp.bfloat16):
    result = spread * jax.random.normal(own_key, shape, jnp.float32)
    if cuts:
        result = result * block_levels(own_key, shape, cuts, -0.22, 0.18)
    return jnp.clip(with_spikes(result, jax.random.fold_in(own_key, 3), *heavy), -most, most).astype(held_as)


def setup_inputs(seed: int = 0) -> dict:
    seeds = jax.random.split(jax.random.key(seed), 2)
    return {
        "factors": noise_with(seeds[0], (NAUX, NOCC, NBF), (NOCC * 8) ** -0.5, 0.1875, ((0, 32), (2, 16)), (0, 2, 32, 2.75)),
    }


def reference(factors):
    block = NBF // N_BASIS
    grouped = factors.reshape(N_AUX, P_DEV * NOCC, NBF)

    def one_block(index):
        def one_group(total, flat):
            own = lax.dynamic_slice_in_dim(flat, (index * block).astype(jnp.int32), block, 1)
            tiles = []
            for s in range(SHIFTS):
                other_index = (index + s) % N_BASIS
                other = lax.dynamic_slice_in_dim(flat, (other_index * block).astype(jnp.int32), block, 1)
                part = lax.dot_general(own, other, (((0,), (0,)), ((), ())), preferred_element_type=jnp.float32)
                tiles.append(part)
            return total + jnp.stack(tiles), None

        start = jnp.zeros((SHIFTS, block, block), jnp.float32)
        total, _ = lax.scan(one_group, start, grouped)
        return total

    stacked = lax.map(one_block, jnp.arange(N_BASIS, dtype=jnp.int32))
    return jnp.transpose(stacked, (1, 0, 2, 3)).reshape(SHIFTS, NBF, block)
```

```python
import jax
import jax.numpy as jnp
from jax import lax
from jax.sharding import Mesh, PartitionSpec as P

SIZES = {"zl": 4, "y": 8, "zh": 2, "x": 4, "c": 2}
AUX = ("zl", "y")
BASIS = ("zh", "x", "c")


def send(value, axes, target):
    sizes = [SIZES[a] for a in axes]
    count = 1
    for size in sizes:
        count *= size

    def coords(index):
        out = []
        for size in reversed(sizes):
            out.append(index % size)
            index //= size
        return tuple(reversed(out))

    def flat(position):
        index = 0
        for size, p in zip(sizes, position):
            index = index * size + p
        return index

    pairs = []
    for i in range(count):
        to = target(*coords(i))
        if to is not None:
            pairs.append((i, flat(to)))
    return lax.ppermute(value, axes, pairs)


def along_x(zh, x, c):
    if c == 0:
        return (zh, x - 1, 0) if x > 0 else None
    return (zh, x + 1, 1) if x < 3 else None


def across_z(zh, x, c):
    if c == 0 and x == 0:
        return (1 - zh, 3, 0)
    if c == 1 and x == 3:
        return (1 - zh, 0, 1)
    return None


def to_previous_chip(zh, x, c):
    if c == 0:
        return None
    return (zh, x - 1, 1) if x > 0 else (1 - zh, 3, 1)


def other_core(c):
    return (1 - c,)


def product(a, b):
    return lax.dot_general(a, b, (((0, 1), (0, 1)), ((), ())), preferred_element_type=jnp.float32)


def code(full, half):
    top = jnp.maximum(jnp.max(jnp.abs(full)), jnp.max(jnp.abs(half)))
    power = jnp.clip(jnp.floor(jnp.log2(jnp.maximum(top, 1e-30))), -100.0, 100.0)
    scale = jnp.exp2(13.0 - power)

    def part(tile):
        cols = tile.shape[1] // 128
        tile = (tile * scale).astype(jnp.float16)
        return tile.reshape(32, 16, cols, 128).transpose(0, 2, 1, 3).reshape(32, 16 * cols, 128)

    return jnp.concatenate([part(full), part(half)], axis=1), power.astype(jnp.float16)


def add_up(parts):
    power = parts[:, -1, 0].astype(jnp.float32)
    return jnp.sum(parts[:, :-8].astype(jnp.float32) * jnp.exp2(power - 13.0)[:, None, None], axis=0)


def rows_of(cols, value):
    return value.reshape(cols, 16, 128).transpose(1, 0, 2).reshape(16, cols * 128)


def on_device(own):
    core = lax.axis_index("c")
    x = lax.axis_index("x")
    crossed = send(own, BASIS, across_z)
    beside = send(own, ("c",), other_core)
    along = send(own, BASIS, along_x)

    first = core == 0
    early_full = product(own, own)
    early_half = lax.cond(
        first,
        lambda: product(own, beside[:, :, :256]),
        lambda: product(beside, own[:, :, 256:]),
    )
    coded, power = code(early_full, early_half)
    coded = coded.reshape(4, 8, 96, 128).transpose(1, 0, 2, 3).reshape(8, 384, 128)
    coded = jnp.concatenate([coded, jnp.broadcast_to(power, (8, 8, 128))], axis=1)
    coded = lax.all_to_all(coded, "y", 0, 0, tiled=True)
    early = add_up(coded).reshape(4, 96, 128)
    early = jnp.sum(lax.all_to_all(early, "zl", 0, 0, tiled=True), axis=0)

    at_end = jnp.where(first, x == 3, x == 0)
    moved = jnp.where(at_end, crossed, along)
    late_full, late_half = lax.cond(
        first,
        lambda: (product(own, moved), product(beside, moved[:, :, :256])),
        lambda: (product(moved, own), product(moved, beside[:, :, 256:])),
    )
    coded, power = code(late_full, late_half)
    coded = jnp.concatenate([coded, jnp.broadcast_to(power, (32, 8, 128))], axis=1)
    coded = lax.all_to_all(coded, AUX, 0, 0, tiled=True)
    late = add_up(coded)

    swapped = send(jnp.where(first, late[64:], early[64:]), ("c",), other_core)
    back = send(late, BASIS, to_previous_chip)

    s0 = rows_of(4, early[:64])
    s1 = rows_of(4, jnp.where(first, jnp.concatenate([early[64:], swapped]), jnp.concatenate([swapped, back[64:]])))
    s2 = rows_of(4, jnp.where(first, late[:64], back[:64]))
    return jnp.stack([s0, s1, s2])


def solution(mesh):
    fine = Mesh(mesh.devices.reshape(tuple(SIZES.values())), tuple(SIZES))
    return jax.shard_map(
        on_device, mesh=fine, in_specs=(P(AUX, None, BASIS),), out_specs=P(None, BASIS + AUX, None), check_vma=False
    )
```

```python
import functools

import jax
import jax.numpy as jnp
from jax import lax
from jax.experimental import pallas as pl
from jax.experimental.pallas import tpu as pltpu
from jax.sharding import Mesh, PartitionSpec as P

SIZES = {"zl": 4, "y": 8, "zh": 2, "x": 4, "c": 2}
AUX = ("zl", "y")
BASIS = ("zh", "x", "c")


def send(value, axes, target):
    sizes = [SIZES[a] for a in axes]
    count = 1
    for size in sizes:
        count *= size

    def coords(index):
        out = []
        for size in reversed(sizes):
            out.append(index % size)
            index //= size
        return tuple(reversed(out))

    def flat(position):
        index = 0
        for size, p in zip(sizes, position):
            index = index * size + p
        return index

    pairs = []
    for i in range(count):
        to = target(*coords(i))
        if to is not None:
            pairs.append((i, flat(to)))
    return lax.ppermute(value, axes, pairs)


def along_x(zh, x, c):
    if c == 0:
        return (zh, x - 1, 0) if x > 0 else None
    return (zh, x + 1, 1) if x < 3 else None


def across_z(zh, x, c):
    if c == 0 and x == 0:
        return (1 - zh, 3, 0)
    if c == 1 and x == 3:
        return (1 - zh, 0, 1)
    return None


def to_previous_chip(zh, x, c):
    if c == 0:
        return None
    return (zh, x - 1, 1) if x > 0 else (1 - zh, 3, 1)


def other_core(c):
    return (1 - c,)


def product(a, b):
    return lax.dot_general(a, b, (((0,), (0,)), ((), ())), preferred_element_type=jnp.float32)


def columns(ref, low=0, high=512):
    return ref[:, :, low:high].reshape(-1, high - low)


def put(out, full, half, place):
    base = 0
    top = jnp.zeros((8, 128), jnp.float32)
    for tile in (full, half):
        cols = tile.shape[1] // 128
        for owner in range(32):
            for r in range(2):
                rows = tile[owner * 16 + r * 8 : owner * 16 + r * 8 + 8]
                for c in range(cols):
                    piece = rows[:, c * 128 : c * 128 + 128]
                    row = base + (r * cols + c) * 8
                    lead, at = place(owner, row)
                    if place(owner, row + 4) == (lead, at + 4):
                        out[lead, at : at + 8, :] = piece
                    else:
                        out[lead, at : at + 4, :] = piece[:4]
                        lead, at = place(owner, row + 4)
                        out[lead, at : at + 4, :] = piece[4:]
                    top = jnp.maximum(top, jnp.abs(piece))
        base += 16 * cols
    return top


def power_of(top):
    top = jnp.max(top, axis=(0, 1), keepdims=True)
    return jnp.clip(jnp.floor(jnp.log2(jnp.maximum(top, 1e-30))), -100.0, 100.0)


def scale_down(out, rows, power):
    out[:, :rows, :] = out[:, :rows, :] * jnp.exp2(13.0 - power)[None]
    out[:, rows : rows + 8, :] = jnp.broadcast_to(power[None], (out.shape[0], 8, 128))


def by_owner(owner, row):
    return owner % 8, owner // 8 * 96 + row


def by_slice(owner, row):
    return row // 12, owner * 12 + row % 12


def by_device(owner, row):
    return owner, row


def early_kernel(flags, own, beside, out, top):
    def form(rows, cols, low, place):
        full = product(columns(own), columns(own))
        half = product(columns(rows), columns(cols, low, low + 256))
        top[...] = put(out, full, half, place)

    for core, blocks in ((0, (own, beside, 0)), (1, (beside, own, 256))):
        for end, place in ((0, by_owner), (1, by_slice)):
            pl.when((flags[0] == core) & (flags[1] == end))(functools.partial(form, *blocks, place))
    scale_down(out, 384, power_of(top[...]))


def late_kernel(place, flags, own, beside, moved, early, out, top, own_here, beside_here, moved_here, arrived):
    cuts = (0, 250, 500)

    def fetch(k, n, source, target):
        rows = pl.ds(cuts[k], cuts[k + 1] - cuts[k])
        return pltpu.make_async_copy(source.at[rows], target.at[rows], arrived.at[k, n])

    for k in (0, 1):
        fetch(k, 0, own, own_here).start()
        fetch(k, 1, moved, moved_here).start()
        fetch(k, 2, beside, beside_here).start()

    def form(core):
        full = half = 0.0
        for k in (0, 1):
            rows = slice(cuts[k], cuts[k + 1])
            fetch(k, 0, own, own_here).wait()
            fetch(k, 1, moved, moved_here).wait()
            mine, other = columns(own_here.at[rows]), columns(moved_here.at[rows])
            full += product(mine, other) if core == 0 else product(other, mine)
            fetch(k, 2, beside, beside_here).wait()
            if core == 0:
                half += product(columns(beside_here.at[rows]), columns(moved_here.at[rows], 0, 256))
            else:
                half += product(columns(moved_here.at[rows]), columns(beside_here.at[rows], 256, 512))
        top[...] = put(out, full, half, place)

    for core in (0, 1):
        pl.when(flags[0] == core)(functools.partial(form, core))
    if place is by_owner:
        scale_down(out, 384, power_of(top[...]))
        return
    scale_down(out, 96, power_of(top[...]))
    sums = early[...]
    power = power_of(jnp.abs(sums))
    sums = sums * jnp.exp2(13.0 - power)
    for owner in range(32):
        out[owner, 104:116, :] = sums[owner * 12 : owner * 12 + 12]
    out[:, 116:, :] = jnp.broadcast_to(power[None], (32, 4, 128))


def call(kernel, shape, flags, *blocks, early=None):
    vmem = pl.BlockSpec(memory_space=pltpu.VMEM)
    blocks = [block.transpose(1, 0, 2) for block in blocks]
    specs = [vmem] * len(blocks)
    scratch = [pltpu.VMEM((8, 128), jnp.float32)]
    if early is not None:
        specs = [pl.BlockSpec(memory_space=pl.ANY)] * len(blocks) + [vmem]
        scratch += [pltpu.VMEM(blocks[0].shape, jnp.bfloat16)] * 3 + [pltpu.SemaphoreType.DMA((2, 3))]
        blocks.append(early)
    return pl.pallas_call(
        kernel,
        out_shape=jax.ShapeDtypeStruct(shape, jnp.float32),
        in_specs=[pl.BlockSpec(memory_space=pltpu.SMEM)] + specs,
        out_specs=vmem,
        scratch_shapes=scratch,
        compiler_params=pltpu.CompilerParams(vmem_limit_bytes=40 << 20),
        cost_estimate=pl.CostEstimate(flops=1_600_000_000, bytes_accessed=8_000_000, transcendentals=0),
    )(flags, *blocks).astype(jnp.float16)


def untiled(value, cols):
    return value.reshape(2, cols // 128, 8, 128).transpose(0, 2, 1, 3).reshape(16, cols)


def unscaled(parts, power):
    return parts.astype(jnp.float32) * jnp.exp2(power.astype(jnp.float32) - 13.0)[:, None, None]


def on_device(own):
    core = lax.axis_index("c")
    x = lax.axis_index("x")
    first = core == 0
    at_end = jnp.where(first, x == 3, x == 0)
    flags = jnp.stack([core, at_end.astype(jnp.int32)])

    crossed = send(own, BASIS, across_z)
    beside = send(own, ("c",), other_core)
    along = send(own, BASIS, along_x)

    def add_over_y(parts):
        parts = lax.all_to_all(parts, "y", 0, 0, tiled=True)
        return jnp.sum(unscaled(parts[:, :384], parts[:, -1, 0]), axis=0)

    def form_early():
        return add_over_y(call(early_kernel, (8, 392, 128), flags, own, beside))

    def late_over_y():
        kernel = functools.partial(late_kernel, by_owner)
        return add_over_y(call(kernel, (8, 392, 128), flags, own, beside, along, early=total))

    def over_z():
        parts = jnp.concatenate([total.reshape(4, 96, 128), late_total.reshape(4, 96, 128)], axis=1)
        parts = jnp.sum(lax.all_to_all(parts, "zl", 0, 0, tiled=True), axis=0)
        return parts[:96], parts[96:]

    def late_over_aux():
        kernel = functools.partial(late_kernel, by_device)
        parts = call(kernel, (32, 120, 128), flags, own, beside, crossed, early=total)
        parts = lax.all_to_all(parts, AUX, 0, 0, tiled=True)
        late = jnp.sum(unscaled(parts[:, :96], parts[:, 103, 0]), axis=0)
        early = unscaled(parts[:, 104:116], parts[:, 119, 0]).reshape(4, 8, 12, 128)
        return jnp.sum(early, axis=0).reshape(96, 128), late

    nothing = lambda: jnp.zeros((384, 128), jnp.float32)
    total = lax.cond(core < 2, form_early, nothing)
    total, along = lax.optimization_barrier((total, along))
    late_total = lax.cond(at_end, nothing, late_over_y)
    late_total, crossed = lax.optimization_barrier((late_total, crossed))
    early, late = lax.cond(at_end, late_over_aux, over_z)

    swapped = send(jnp.where(first, late[64:], early[64:]), ("c",), other_core)
    back = send(late, BASIS, to_previous_chip)

    s0 = untiled(early[:64], 512)
    left = untiled(jnp.where(first, early[64:], swapped), 256)
    right = untiled(jnp.where(first, swapped, back[64:]), 256)
    s1 = jnp.concatenate([left, right], axis=1)
    s2 = untiled(jnp.where(first, late[:64], back[:64]), 512)
    return jnp.stack([s0, s1, s2])


def solution(mesh):
    fine = Mesh(mesh.devices.reshape(tuple(SIZES.values())), tuple(SIZES))
    return jax.shard_map(
        on_device, mesh=fine, in_specs=(P(AUX, None, BASIS),), out_specs=P(None, BASIS + AUX, None), check_vma=False
    )
```

```python
import functools

import jax
import jax.numpy as jnp
from jax import lax
from jax.experimental import pallas as pl
from jax.experimental.pallas import tpu as pltpu
from jax.sharding import Mesh, PartitionSpec as P

SIZES = {"zl": 4, "y": 8, "zh": 2, "x": 4, "c": 2}
AUX = ("zl", "y")
BASIS = ("zh", "x", "c")


def send(value, axes, target):
    sizes = [SIZES[a] for a in axes]
    count = 1
    for size in sizes:
        count *= size

    def coords(index):
        out = []
        for size in reversed(sizes):
            out.append(index % size)
            index //= size
        return tuple(reversed(out))

    def flat(position):
        index = 0
        for size, p in zip(sizes, position):
            index = index * size + p
        return index

    pairs = []
    for i in range(count):
        to = target(*coords(i))
        if to is not None:
            pairs.append((i, flat(to)))
    return lax.ppermute(value, axes, pairs)


def along_x(zh, x, c):
    if c == 0:
        return (zh, x - 1, 0) if x > 0 else None
    return (zh, x + 1, 1) if x < 3 else None


def across_z(zh, x, c):
    if c == 0 and x == 0:
        return (1 - zh, 3, 0)
    if c == 1 and x == 3:
        return (1 - zh, 0, 1)
    return None


def to_previous_chip(zh, x, c):
    if c == 0:
        return None
    return (zh, x - 1, 1) if x > 0 else (1 - zh, 3, 1)


def other_core(c):
    return (1 - c,)


def product(a, b):
    return lax.dot_general(a, b, (((0,), (0,)), ((), ())), preferred_element_type=jnp.float32)


def columns(ref, low=0, high=512):
    return ref[:, :, low:high].reshape(-1, high - low)


def put(out, tile, place, base, cols, row_low=0, col_low=0):
    top = jnp.zeros((8, 128), jnp.float32)
    for low in range(0, tile.shape[0], 8):
        owner, r = (row_low + low) // 16, (row_low + low) // 8 % 2
        for at_col in range(0, tile.shape[1], 128):
            piece = tile[low : low + 8, at_col : at_col + 128]
            row = base + (r * cols + col_low + at_col) // 128 * 8
            lead, at = place(owner, row)
            if place(owner, row + 4) == (lead, at + 4):
                out[lead, at : at + 8, :] = piece
            else:
                out[lead, at : at + 4, :] = piece[:4]
                lead, at = place(owner, row + 4)
                out[lead, at : at + 4, :] = piece[4:]
            top = jnp.maximum(top, jnp.abs(piece))
    return top


def power_of(top):
    top = jnp.max(top, axis=(0, 1), keepdims=True)
    return jnp.clip(jnp.floor(jnp.log2(jnp.maximum(top, 1e-30))), -100.0, 100.0)


def by_slice(owner, row):
    if row < 64:
        return row // 8, owner * 12 + row % 8
    return (row - 64) // 4, owner * 12 + 8 + row % 4


def by_owner(owner, row):
    return owner % 8, owner // 8 * 192 + row


def by_device(owner, row):
    return owner, row


def early_half(core, own, beside):
    if core == 0:
        return product(columns(own), columns(beside, 0, 256))
    return product(columns(beside), columns(own, 256, 512))


def finish(out, rows, top):
    power = power_of(top)
    out[:, :rows, :] = out[:, :rows, :] * jnp.exp2(13.0 - power)[None]
    return power[None]


def early_kernel(flags, own, beside, out, top):
    def form(core):
        largest = put(out, product(columns(own), columns(own)), by_slice, 0, 512)
        top[...] = jnp.maximum(largest, put(out, early_half(core, own, beside), by_slice, 64, 256))

    for core in (0, 1):
        pl.when(flags[0] == core)(functools.partial(form, core))
    out[:, 384:, :] = jnp.broadcast_to(finish(out, 384, top[...]), (8, 8, 128))


def late_kernel(flags, own, beside, moved, *rest):
    out, top, own_here, beside_here, moved_here, arrived = rest[-6:]
    early = rest[0] if len(rest) == 7 else None
    place, base = (by_owner, 96) if early is None else (by_device, 0)

    def fetch(n, source, target, low, high):
        return pltpu.make_async_copy(source.at[:, :, low:high], target.at[:, :, low:high], arrived.at[n])

    copies = [
        fetch(0, own, own_here, 0, 512),
        fetch(1, moved, moved_here, 0, 256),
        fetch(2, moved, moved_here, 256, 512),
        fetch(3, beside, beside_here, 0, 512),
    ]
    for copy in copies:
        copy.start()

    def form(core):
        copies[0].wait()
        tops = []
        if early is None:
            tops.append(put(out, product(columns(own_here), columns(own_here)), place, 0, 512))
        for n, low in ((1, 0), (2, 256)):
            copies[n].wait()
            part = columns(moved_here, low, low + 256)
            if core == 0:
                tops.append(put(out, product(columns(own_here), part), place, base, 512, col_low=low))
            else:
                tops.append(put(out, product(part, columns(own_here)), place, base, 512, row_low=low))
        copies[3].wait()
        if core == 0:
            half = product(columns(beside_here), columns(moved_here, 0, 256))
        else:
            half = product(columns(moved_here), columns(beside_here, 256, 512))
        tops.append(put(out, half, place, base + 64, 256))
        if early is None:
            tops.append(put(out, early_half(core, own_here, beside_here), place, 64, 256))
        top[...] = functools.reduce(jnp.maximum, tops)

    for core in (0, 1):
        pl.when(flags[0] == core)(functools.partial(form, core))
    if early is None:
        out[:, 768:, :] = jnp.broadcast_to(finish(out, 768, top[...]), (8, 8, 128))
        return
    out[:, 108:110, :] = jnp.broadcast_to(finish(out, 96, top[...]), (32, 2, 128))
    sums = early[...]
    power = power_of(jnp.max(jnp.abs(sums), axis=0))
    out[:, 96:108, :] = sums * jnp.exp2(13.0 - power)[None]
    out[:, 110:, :] = jnp.broadcast_to(power[None], (32, 2, 128))


def call(kernel, shape, flags, blocks, early=()):
    vmem = pl.BlockSpec(memory_space=pltpu.VMEM)
    blocks = [block.transpose(1, 0, 2) for block in blocks]
    specs = [vmem] * len(blocks)
    scratch = [pltpu.VMEM((8, 128), jnp.float32)]
    if kernel is late_kernel:
        specs = [pl.BlockSpec(memory_space=pl.ANY)] * len(blocks) + [vmem] * len(early)
        scratch += [pltpu.VMEM(blocks[0].shape, jnp.bfloat16)] * 3 + [pltpu.SemaphoreType.DMA((4,))]
    return pl.pallas_call(
        kernel,
        out_shape=jax.ShapeDtypeStruct(shape, jnp.float32),
        in_specs=[pl.BlockSpec(memory_space=pltpu.SMEM)] + specs,
        out_specs=vmem,
        scratch_shapes=scratch,
        compiler_params=pltpu.CompilerParams(vmem_limit_bytes=40 << 20),
        cost_estimate=pl.CostEstimate(flops=1_600_000_000, bytes_accessed=8_000_000, transcendentals=0),
    )(flags, *blocks, *early).astype(jnp.float16)


def untiled(value, cols):
    return value.reshape(2, cols // 128, 8, 128).transpose(0, 2, 1, 3).reshape(16, cols)


def unscaled(parts, power):
    return parts.astype(jnp.float32) * jnp.exp2(power.astype(jnp.float32) - 13.0)[:, None, None]


def on_device(own):
    core = lax.axis_index("c")
    x = lax.axis_index("x")
    first = core == 0
    at_end = jnp.where(first, x == 3, x == 0)
    flags = jnp.stack([core, core])

    kind = jnp.where(at_end, 2, jnp.where((x == 0) | (x == 3), 1, 0))

    along = send(own, BASIS, along_x)
    crossed = send(own, BASIS, across_z)

    def zeros(*shapes):
        return tuple(jnp.zeros(shape + (128,), jnp.float32) for shape in shapes)

    def sum_over_y(parts):
        parts = lax.all_to_all(parts, "y", 0, 0, tiled=True)
        return jnp.sum(unscaled(parts[:, :-8], parts[:, -1, 0]), axis=0)

    def form_early():
        beside = send(own, ("c",), other_core)
        (sums,) = lax.cond(
            kind == 1,
            lambda: zeros((384,)),
            lambda: (sum_over_y(call(early_kernel, (8, 392, 128), flags, (own, beside))),),
        )
        return sums.reshape(32, 12, 128), beside

    def late_over_aux(moved):
        parts = call(late_kernel, (32, 112, 128), flags, (own, beside, moved), (early_sums,))
        parts = lax.all_to_all(parts, AUX, 0, 0, tiled=True)
        late = jnp.sum(unscaled(parts[:, :96], parts[:, 108, 0]), axis=0)
        early = jnp.sum(unscaled(parts[:, 96:108], parts[:, 110, 0]).reshape(4, 8, 12, 128), axis=0)
        return jnp.concatenate([early[:, :8].reshape(64, 128), early[:, 8:].reshape(32, 128), late])

    def all_over_y():
        return sum_over_y(call(late_kernel, (8, 776, 128), flags, (own, beside, along)))

    def over_z():
        return jnp.sum(lax.all_to_all(sums_y.reshape(4, 192, 128), "zl", 0, 0, tiled=True), axis=0)

    early_sums, beside = lax.cond(core < 2, form_early, lambda: zeros((32, 12)) + (own,))
    early_sums, along = lax.optimization_barrier((early_sums, along))
    sums, sums_y = lax.switch(
        kind,
        [
            lambda: (late_over_aux(along),) + zeros((768,)),
            lambda: zeros((192,)) + (all_over_y(),),
            lambda: zeros((192,), (768,)),
        ],
    )
    sums, sums_y, crossed = lax.optimization_barrier((sums, sums_y, crossed))
    sums = lax.switch(kind, [lambda: sums, over_z, lambda: late_over_aux(crossed)])
    early, late = sums[:96], sums[96:]

    swapped = send(jnp.where(first, late[64:], early[64:]), ("c",), other_core)
    back = send(late, BASIS, to_previous_chip)

    s0 = untiled(early[:64], 512)
    left = untiled(jnp.where(first, early[64:], swapped), 256)
    right = untiled(jnp.where(first, swapped, back[64:]), 256)
    s1 = jnp.concatenate([left, right], axis=1)
    s2 = untiled(jnp.where(first, late[:64], back[:64]), 512)
    return jnp.stack([s0, s1, s2])


def solution(mesh):
    fine = Mesh(mesh.devices.reshape(tuple(SIZES.values())), tuple(SIZES))
    return jax.shard_map(
        on_device, mesh=fine, in_specs=(P(AUX, None, BASIS),), out_specs=P(None, BASIS + AUX, None), check_vma=False
    )
```

```python
import functools

import jax
import jax.numpy as jnp
from jax import lax
from jax.experimental import pallas as pl
from jax.experimental.pallas import tpu as pltpu
from jax.sharding import Mesh, PartitionSpec as P

SIZES = {"zl": 4, "y": 8, "zh": 2, "x": 4, "c": 2}
AUX = ("zl", "y")
BASIS = ("zh", "x", "c")


def send(value, axes, target):
    sizes = [SIZES[a] for a in axes]
    count = 1
    for size in sizes:
        count *= size

    def coords(index):
        out = []
        for size in reversed(sizes):
            out.append(index % size)
            index //= size
        return tuple(reversed(out))

    def flat(position):
        index = 0
        for size, p in zip(sizes, position):
            index = index * size + p
        return index

    pairs = []
    for i in range(count):
        to = target(*coords(i))
        if to is not None:
            pairs.append((i, flat(to)))
    return lax.ppermute(value, axes, pairs)


def along_x(zh, x, c):
    if c == 0:
        return (zh, x - 1, 0) if x > 0 else None
    return (zh, x + 1, 1) if x < 3 else None


def across_z(zh, x, c):
    if c == 0 and x == 0:
        return (1 - zh, 3, 0)
    if c == 1 and x == 3:
        return (1 - zh, 0, 1)
    return None


def to_previous_chip(zh, x, c):
    if c == 0:
        return None
    return (zh, x - 1, 1) if x > 0 else (1 - zh, 3, 1)


def other_core(c):
    return (1 - c,)


def product(a, b):
    return lax.dot_general(a, b, (((0,), (0,)), ((), ())), preferred_element_type=jnp.float32)


def columns(ref, low=0, high=512):
    return ref[:, :, low:high].reshape(-1, high - low)


def put(out, tile, place, base, cols, row_low=0, col_low=0):
    top = jnp.zeros((8, 128), jnp.float32)
    for low in range(0, tile.shape[0], 8):
        owner, r = (row_low + low) // 16, (row_low + low) // 8 % 2
        for at_col in range(0, tile.shape[1], 128):
            piece = tile[low : low + 8, at_col : at_col + 128]
            row = base + (r * cols + col_low + at_col) // 128 * 8
            lead, at = place(owner, row)
            if place(owner, row + 4) == (lead, at + 4):
                out[lead, at : at + 8, :] = piece
            else:
                out[lead, at : at + 4, :] = piece[:4]
                lead, at = place(owner, row + 4)
                out[lead, at : at + 4, :] = piece[4:]
            top = jnp.maximum(top, jnp.abs(piece))
    return top


def power_of(top):
    top = jnp.max(top, axis=(0, 1), keepdims=True)
    return jnp.clip(jnp.floor(jnp.log2(jnp.maximum(top, 1e-30))), -100.0, 100.0)


def by_slice(owner, row):
    if row < 64:
        return row // 8, owner * 12 + row % 8
    return (row - 64) // 4, owner * 12 + 8 + row % 4


def by_owner(owner, row):
    return owner % 8, owner // 8 * 192 + row


def by_device(owner, row):
    return owner, row


def early_half(core, own, beside):
    if core == 0:
        return product(columns(own), columns(beside, 0, 256))
    return product(columns(beside), columns(own, 256, 512))


def coded(value, power):
    value = value * jnp.exp2(6.0 - power)[None]
    return value * jnp.abs(value)


def finish(out, rows, top):
    power = power_of(top)
    out[:, :rows, :] = coded(out[:, :rows, :], power)
    return power[None]


def early_kernel(flags, own, beside, out, top):
    def form(core):
        largest = put(out, product(columns(own), columns(own)), by_slice, 0, 512)
        top[...] = jnp.maximum(largest, put(out, early_half(core, own, beside), by_slice, 64, 256))

    for core in (0, 1):
        pl.when(flags[0] == core)(functools.partial(form, core))
    out[:, 384:, :] = jnp.broadcast_to(finish(out, 384, top[...]), (8, 8, 128))


def late_kernel(flags, own, beside, moved, *rest):
    out, top, own_here, beside_here, moved_here, arrived = rest[-6:]
    early = rest[0] if len(rest) == 7 else None
    place, base = (by_owner, 96) if early is None else (by_device, 0)

    def fetch(n, source, target, low, high):
        return pltpu.make_async_copy(source.at[:, :, low:high], target.at[:, :, low:high], arrived.at[n])

    copies = [
        fetch(0, own, own_here, 0, 512),
        fetch(1, moved, moved_here, 0, 256),
        fetch(2, moved, moved_here, 256, 512),
        fetch(3, beside, beside_here, 0, 512),
    ]
    for copy in copies:
        copy.start()

    def form(core):
        copies[0].wait()
        tops = []
        if early is None:
            tops.append(put(out, product(columns(own_here), columns(own_here)), place, 0, 512))
        for n, low in ((1, 0), (2, 256)):
            copies[n].wait()
            part = columns(moved_here, low, low + 256)
            if core == 0:
                tops.append(put(out, product(columns(own_here), part), place, base, 512, col_low=low))
            else:
                tops.append(put(out, product(part, columns(own_here)), place, base, 512, row_low=low))
        copies[3].wait()
        if core == 0:
            half = product(columns(beside_here), columns(moved_here, 0, 256))
        else:
            half = product(columns(moved_here), columns(beside_here, 256, 512))
        tops.append(put(out, half, place, base + 64, 256))
        if early is None:
            tops.append(put(out, early_half(core, own_here, beside_here), place, 64, 256))
        top[...] = functools.reduce(jnp.maximum, tops)

    for core in (0, 1):
        pl.when(flags[0] == core)(functools.partial(form, core))
    if early is None:
        out[:, 768:, :] = jnp.broadcast_to(finish(out, 768, top[...]), (8, 8, 128))
        return
    out[:, 108:110, :] = jnp.broadcast_to(finish(out, 96, top[...]), (32, 2, 128))
    sums = early[...]
    power = power_of(jnp.max(jnp.abs(sums), axis=0))
    out[:, 96:108, :] = coded(sums, power)
    out[:, 110:, :] = jnp.broadcast_to(power[None], (32, 2, 128))


def call(kernel, shape, flags, blocks, early=()):
    vmem = pl.BlockSpec(memory_space=pltpu.VMEM)
    blocks = [block.transpose(1, 0, 2) for block in blocks]
    specs = [vmem] * len(blocks)
    scratch = [pltpu.VMEM((8, 128), jnp.float32)]
    if kernel is late_kernel:
        specs = [pl.BlockSpec(memory_space=pl.ANY)] * len(blocks) + [vmem] * len(early)
        scratch += [pltpu.VMEM(blocks[0].shape, jnp.bfloat16)] * 3 + [pltpu.SemaphoreType.DMA((4,))]
    return pl.pallas_call(
        kernel,
        out_shape=jax.ShapeDtypeStruct(shape, jnp.float32),
        in_specs=[pl.BlockSpec(memory_space=pltpu.SMEM)] + specs,
        out_specs=vmem,
        scratch_shapes=scratch,
        compiler_params=pltpu.CompilerParams(vmem_limit_bytes=40 << 20),
        cost_estimate=pl.CostEstimate(flops=1_600_000_000, bytes_accessed=8_000_000, transcendentals=0),
    )(flags, *blocks, *early).astype(jnp.float16)


def untiled(value, cols):
    return value.reshape(2, cols // 128, 8, 128).transpose(0, 2, 1, 3).reshape(16, cols)


def decoded(parts, power):
    parts = parts.astype(jnp.float32)
    value = parts * lax.rsqrt(jnp.maximum(jnp.abs(parts), 1e-30))
    return value * jnp.exp2(power.astype(jnp.float32) - 6.0)[:, None, None]


def on_device(own):
    core = lax.axis_index("c")
    x = lax.axis_index("x")
    first = core == 0
    at_end = jnp.where(first, x == 3, x == 0)
    flags = jnp.stack([core, core])

    kind = jnp.where(at_end, 2, jnp.where((x == 0) | (x == 3), 1, 0))

    along = send(own, BASIS, along_x)
    crossed = send(own, BASIS, across_z)

    def zeros(*shapes):
        return tuple(jnp.zeros(shape + (128,), jnp.float32) for shape in shapes)

    def sum_over_y(parts):
        parts = lax.all_to_all(parts, "y", 0, 0, tiled=True)
        return jnp.sum(decoded(parts[:, :-8], parts[:, -1, 0]), axis=0)

    def form_early():
        beside = send(own, ("c",), other_core)
        (sums,) = lax.cond(
            kind == 1,
            lambda: zeros((384,)),
            lambda: (sum_over_y(call(early_kernel, (8, 392, 128), flags, (own, beside))),),
        )
        return sums.reshape(32, 12, 128), beside

    def late_over_aux(moved):
        parts = call(late_kernel, (32, 112, 128), flags, (own, beside, moved), (early_sums,))
        parts = lax.all_to_all(parts, AUX, 0, 0, tiled=True)
        late = jnp.sum(decoded(parts[:, :96], parts[:, 108, 0]), axis=0)
        early = jnp.sum(decoded(parts[:, 96:108], parts[:, 110, 0]).reshape(4, 8, 12, 128), axis=0)
        return jnp.concatenate([early[:, :8].reshape(64, 128), early[:, 8:].reshape(32, 128), late])

    def all_over_y():
        return sum_over_y(call(late_kernel, (8, 776, 128), flags, (own, beside, along)))

    def over_z():
        return jnp.sum(lax.all_to_all(sums_y.reshape(4, 192, 128), "zl", 0, 0, tiled=True), axis=0)

    early_sums, beside = lax.cond(core < 2, form_early, lambda: zeros((32, 12)) + (own,))
    early_sums, along = lax.optimization_barrier((early_sums, along))
    sums, sums_y = lax.switch(
        kind,
        [
            lambda: (late_over_aux(along),) + zeros((768,)),
            lambda: zeros((192,)) + (all_over_y(),),
            lambda: zeros((192,), (768,)),
        ],
    )
    sums, sums_y, crossed = lax.optimization_barrier((sums, sums_y, crossed))
    sums = lax.switch(kind, [lambda: sums, over_z, lambda: late_over_aux(crossed)])
    early, late = sums[:96], sums[96:]

    swapped = send(jnp.where(first, late[64:], early[64:]), ("c",), other_core)
    back = send(late, BASIS, to_previous_chip)

    s0 = untiled(early[:64], 512)
    left = untiled(jnp.where(first, early[64:], swapped), 256)
    right = untiled(jnp.where(first, swapped, back[64:]), 256)
    s1 = jnp.concatenate([left, right], axis=1)
    s2 = untiled(jnp.where(first, late[:64], back[:64]), 512)
    return jnp.stack([s0, s1, s2])


def solution(mesh):
    fine = Mesh(mesh.devices.reshape(tuple(SIZES.values())), tuple(SIZES))
    return jax.shard_map(
        on_device, mesh=fine, in_specs=(P(AUX, None, BASIS),), out_specs=P(None, BASIS + AUX, None), check_vma=False
    )
```

```python
import functools

import jax
import jax.numpy as jnp
from jax import lax
from jax.experimental import pallas as pl
from jax.experimental.pallas import tpu as pltpu
from jax.sharding import Mesh, PartitionSpec as P

SIZES = {"zl": 4, "y": 8, "zh": 2, "x": 4, "c": 2}
AUX = ("zl", "y")
BASIS = ("zh", "x", "c")


def send(value, axes, target):
    sizes = [SIZES[a] for a in axes]
    count = 1
    for size in sizes:
        count *= size

    def coords(index):
        out = []
        for size in reversed(sizes):
            out.append(index % size)
            index //= size
        return tuple(reversed(out))

    def flat(position):
        index = 0
        for size, p in zip(sizes, position):
            index = index * size + p
        return index

    pairs = []
    for i in range(count):
        to = target(*coords(i))
        if to is not None:
            pairs.append((i, flat(to)))
    return lax.ppermute(value, axes, pairs)


def along_x(zh, x, c):
    if c == 0:
        return (zh, x - 1, 0) if x > 0 else None
    return (zh, x + 1, 1) if x < 3 else None


def across_z(zh, x, c):
    if c == 0 and x == 0:
        return (1 - zh, 3, 0)
    if c == 1 and x == 3:
        return (1 - zh, 0, 1)
    return None


def to_previous_chip(zh, x, c):
    if c == 0:
        return None
    return (zh, x - 1, 1) if x > 0 else (1 - zh, 3, 1)


def other_core(c):
    return (1 - c,)


def product(a, b):
    return lax.dot_general(a, b, (((0,), (0,)), ((), ())), preferred_element_type=jnp.float32)


def columns(ref, low=0, high=512):
    return ref[:, :, low:high].reshape(-1, high - low)


def put(out, tile, place, base, cols, row_low=0, col_low=0):
    tops = [jnp.zeros((8, 128), jnp.float32)] * 4
    for low in range(0, tile.shape[0], 8):
        owner, r = (row_low + low) // 16, (row_low + low) // 8 % 2
        for at_col in range(0, tile.shape[1], 128):
            piece = tile[low : low + 8, at_col : at_col + 128]
            row = base + (r * cols + col_low + at_col) // 128 * 8
            lead, at = place(owner, row)
            if place(owner, row + 4) == (lead, at + 4):
                out[lead, at : at + 8, :] = piece
            else:
                out[lead, at : at + 4, :] = piece[:4]
                lead, at = place(owner, row + 4)
                out[lead, at : at + 4, :] = piece[4:]
            tops = tops[1:] + [jnp.maximum(tops[0], jnp.abs(piece))]
    return functools.reduce(jnp.maximum, tops)


def power_of(top):
    top = jnp.max(top, axis=(0, 1), keepdims=True)
    return jnp.clip(jnp.floor(jnp.log2(jnp.maximum(top, 1e-30))), -100.0, 100.0)


def by_slice(owner, row):
    if row < 64:
        return row // 8, owner * 12 + row % 8
    return (row - 64) // 4, owner * 12 + 8 + row % 4


def by_owner(owner, row):
    return owner % 8, owner // 8 * 192 + row


def by_device(owner, row):
    return owner, row


def early_half(core, own, beside):
    if core == 0:
        return product(columns(own), columns(beside, 0, 256))
    return product(columns(beside), columns(own, 256, 512))


def coded(value, power):
    value = value * jnp.exp2(6.0 - power)[None]
    return value * jnp.abs(value)


def finish(out, rows, top):
    power = power_of(top)
    out[:, :rows, :] = coded(out[:, :rows, :], power)
    return power[None]


def early_kernel(flags, own, beside, out, top):
    def form(core):
        largest = put(out, product(columns(own), columns(own)), by_slice, 0, 512)
        top[...] = jnp.maximum(largest, put(out, early_half(core, own, beside), by_slice, 64, 256))

    for core in (0, 1):
        pl.when(flags[0] == core)(functools.partial(form, core))
    out[:, 384:, :] = jnp.broadcast_to(finish(out, 384, top[...]), (8, 8, 128))


def late_kernel(flags, own, beside, moved, *rest):
    out, top, own_here, beside_here, moved_here, arrived = rest[-6:]
    early = rest[0] if len(rest) == 7 else None
    place, base = (by_owner, 96) if early is None else (by_device, 0)

    def fetch(n, source, target, low, high):
        return pltpu.make_async_copy(source.at[:, :, low:high], target.at[:, :, low:high], arrived.at[n])

    copies = [
        fetch(0, own, own_here, 0, 512),
        fetch(1, moved, moved_here, 0, 256),
        fetch(2, moved, moved_here, 256, 512),
        fetch(3, beside, beside_here, 0, 512),
    ]
    for copy in copies:
        copy.start()

    def form(core):
        copies[0].wait()
        tops = []
        if early is None:
            tops.append(put(out, product(columns(own_here), columns(own_here)), place, 0, 512))
        for n, low in ((1, 0), (2, 256)):
            copies[n].wait()
            part = columns(moved_here, low, low + 256)
            if core == 0:
                tops.append(put(out, product(columns(own_here), part), place, base, 512, col_low=low))
            else:
                tops.append(put(out, product(part, columns(own_here)), place, base, 512, row_low=low))
        copies[3].wait()
        if core == 0:
            half = product(columns(beside_here), columns(moved_here, 0, 256))
        else:
            half = product(columns(moved_here), columns(beside_here, 256, 512))
        tops.append(put(out, half, place, base + 64, 256))
        if early is None:
            tops.append(put(out, early_half(core, own_here, beside_here), place, 64, 256))
        top[...] = functools.reduce(jnp.maximum, tops)

    for core in (0, 1):
        pl.when(flags[0] == core)(functools.partial(form, core))
    if early is None:
        out[:, 768:, :] = jnp.broadcast_to(finish(out, 768, top[...]), (8, 8, 128))
        return
    out[:, 108:110, :] = jnp.broadcast_to(finish(out, 96, top[...]), (32, 2, 128))
    sums = early[...]
    power = power_of(jnp.max(jnp.abs(sums), axis=0))
    out[:, 96:108, :] = coded(sums, power)
    out[:, 110:, :] = jnp.broadcast_to(power[None], (32, 2, 128))


def call(kernel, shape, flags, blocks, early=()):
    vmem = pl.BlockSpec(memory_space=pltpu.VMEM)
    blocks = [block.transpose(1, 0, 2) for block in blocks]
    specs = [vmem] * len(blocks)
    scratch = [pltpu.VMEM((8, 128), jnp.float32)]
    if kernel is late_kernel:
        specs = [pl.BlockSpec(memory_space=pl.ANY)] * len(blocks) + [vmem] * len(early)
        scratch += [pltpu.VMEM(blocks[0].shape, jnp.bfloat16)] * 3 + [pltpu.SemaphoreType.DMA((4,))]
    return pl.pallas_call(
        kernel,
        out_shape=jax.ShapeDtypeStruct(shape, jnp.float32),
        in_specs=[pl.BlockSpec(memory_space=pltpu.SMEM)] + specs,
        out_specs=vmem,
        scratch_shapes=scratch,
        compiler_params=pltpu.CompilerParams(vmem_limit_bytes=40 << 20),
        cost_estimate=pl.CostEstimate(flops=1_600_000_000, bytes_accessed=8_000_000, transcendentals=0),
    )(flags, *blocks, *early).astype(jnp.float16)


def untiled(value, cols):
    return value.reshape(2, cols // 128, 8, 128).transpose(0, 2, 1, 3).reshape(16, cols)


def decoded(parts, power):
    parts = parts.astype(jnp.float32)
    value = parts * lax.rsqrt(jnp.maximum(jnp.abs(parts), 1e-30))
    return value * jnp.exp2(power.astype(jnp.float32) - 6.0)[:, None, None]


def on_device(own):
    core = lax.axis_index("c")
    x = lax.axis_index("x")
    first = core == 0
    at_end = jnp.where(first, x == 3, x == 0)
    flags = jnp.stack([core, core])

    kind = jnp.where(at_end, 2, jnp.where((x == 0) | (x == 3), 1, 0))

    along = send(own, BASIS, along_x)
    crossed = send(own, BASIS, across_z)

    def zeros(*shapes):
        return tuple(jnp.zeros(shape + (128,), jnp.float32) for shape in shapes)

    def sum_over_y(parts):
        parts = lax.all_to_all(parts, "y", 0, 0, tiled=True)
        return jnp.sum(decoded(parts[:, :-8], parts[:, -1, 0]), axis=0)

    def form_early():
        beside = send(own, ("c",), other_core)
        (sums,) = lax.cond(
            kind == 1,
            lambda: zeros((384,)),
            lambda: (sum_over_y(call(early_kernel, (8, 392, 128), flags, (own, beside))),),
        )
        return sums.reshape(32, 12, 128), beside

    def late_over_aux(moved):
        parts = call(late_kernel, (32, 112, 128), flags, (own, beside, moved), (early_sums,))
        parts = lax.all_to_all(parts, AUX, 0, 0, tiled=True)
        late = jnp.sum(decoded(parts[:, :96], parts[:, 108, 0]), axis=0)
        early = jnp.sum(decoded(parts[:, 96:108], parts[:, 110, 0]).reshape(4, 8, 12, 128), axis=0)
        return jnp.concatenate([early[:, :8].reshape(64, 128), early[:, 8:].reshape(32, 128), late])

    def all_over_y():
        return sum_over_y(call(late_kernel, (8, 776, 128), flags, (own, beside, along)))

    def over_z():
        return jnp.sum(lax.all_to_all(sums_y.reshape(4, 192, 128), "zl", 0, 0, tiled=True), axis=0)

    early_sums, beside = lax.cond(core < 2, form_early, lambda: zeros((32, 12)) + (own,))
    early_sums, along = lax.optimization_barrier((early_sums, along))
    sums, sums_y = lax.switch(
        kind,
        [
            lambda: (late_over_aux(along),) + zeros((768,)),
            lambda: zeros((192,)) + (all_over_y(),),
            lambda: zeros((192,), (768,)),
        ],
    )
    sums, sums_y, crossed = lax.optimization_barrier((sums, sums_y, crossed))
    sums = lax.switch(kind, [lambda: sums, over_z, lambda: late_over_aux(crossed)])
    early, late = sums[:96], sums[96:]

    swapped = send(jnp.where(first, late[64:], early[64:]), ("c",), other_core)
    back = send(late, BASIS, to_previous_chip)

    s0 = untiled(early[:64], 512)
    left = untiled(jnp.where(first, early[64:], swapped), 256)
    right = untiled(jnp.where(first, swapped, back[64:]), 256)
    s1 = jnp.concatenate([left, right], axis=1)
    s2 = untiled(jnp.where(first, late[:64], back[:64]), 512)
    return jnp.stack([s0, s1, s2])


def solution(mesh):
    fine = Mesh(mesh.devices.reshape(tuple(SIZES.values())), tuple(SIZES))
    return jax.shard_map(
        on_device, mesh=fine, in_specs=(P(AUX, None, BASIS),), out_specs=P(None, BASIS + AUX, None), check_vma=False
    )
```
